32 devices in a mesh: dom: 8 (over z, core), leaf: 4 (over y, x).
Axes of the slice: x: 2, y: 2, z: 4, core: 2. Of those that a mesh axis runs over, the one named last changes fastest.
Arguments:
- sources: bfloat16 [32, 196608], P(None, ('dom', 'leaf')), may hold values from -6 to 6
- points: bfloat16 [3, 196608], P(None, ('dom', 'leaf')), may hold values from -4 to 4
- basis: bfloat16 [768, 64, 256], P(('dom', 'leaf')), may hold values from -0.375 to 0.375
- transfer_one: bfloat16 [768, 4096], P(('dom', 'leaf')), may hold values from -0.5 to 0.5
- transfer_two: bfloat16 [384, 4096], P(('dom', 'leaf')), may hold values from -0.5 to 0.5
- near_list: int32 [768, 16], P(('dom', 'leaf')), may hold values from -1 to 767, as said below
- couple_zero: bfloat16 [768, 32, 4096], P(('dom', 'leaf')), may hold values from -0.125 to 0.125
- couple_one: bfloat16 [384, 32, 4096], P(('dom', 'leaf')), may hold values from -0.125 to 0.125
- couple_two: bfloat16 [192, 32, 4096], P(('dom', 'leaf')), may hold values from -0.125 to 0.125
- list_zero: int32 [768, 32], P(('dom', 'leaf')), may hold values from -1 to 767, as said below
- list_one: int32 [384, 32], P(('dom', 'leaf')), may hold values from -1 to 383, as said below
- list_two: int32 [192, 32], P(('dom', 'leaf')), may hold values from -1 to 191, as said below
Outputs:
- product: bfloat16 [32, 196608], P(None, ('dom', 'leaf'))
The draws below stay inside these ranges and needn't reach their ends.
Inputs may be any that keep to these rules, and one draw needn't show every extreme that they name: `near_list`: row b holds leaf b itself first, then distinct other leaves within 24 positions of b; -1 marks empty slots, which come last. `list_zero`: row b holds distinct leaves other than b whose subdomain differs from b's by at most one, a subdomain being the leaves of one index of the dom axis; -1 marks empty slots, which come last. `list_one`: as for list_zero, with the boxes of level one. `list_two`: as for list_zero, with the boxes of level two.
All inputs are finite; a program needn't handle non-finite values.
Results may differ from the reference program's by a relative error of at most 0.0061.
Values may be sent and summed in bfloat16 or wider, within the bound.
No kernel may reach another device: no remote copies, remote signals or barrier semaphores. Data moves between devices by JAX's collectives and lax.ppermute only.
A program may use at most 128 MiB of HBM per device.

```python
import math
import jax
import jax.numpy as jnp
from jax import lax

LEAF_DEV = 24
LEAFPTS = 256
RANK = 64
RHS = 32
NEAR = 16
CSLOTS = 32
NLEAF = 768
NPTS = 196608
NBOX1 = 384
NBOX2 = 192
N_LEAF = 4


def pick_slots(key, first_candidate, candidate_count, slot_count, least, force_last):
    boxes = first_candidate.shape[0]
    box_ids = jnp.arange(boxes, dtype=jnp.int32)
    offsets = jnp.arange(candidate_count, dtype=jnp.int32)
    candidates = first_candidate[:, None] + offsets[None, :]
    usable = (candidates >= 0) & (candidates < boxes) & (candidates != box_ids[:, None])
    key_noise, key_count = jax.random.split(key)
    noise_bits = jax.random.randint(key_noise, (boxes, candidate_count), 0, 65536)
    scores = jnp.where(usable, noise_bits * candidate_count + offsets[None, :], 1 << 30)
    if force_last:
        pinned = (box_ids[:, None] == boxes - 2) & (candidates == boxes - 1)
        scores = jnp.where(pinned, -1, scores)
    ranking = jnp.argsort(scores, axis=1, stable=True)[:, :slot_count]
    chosen = jnp.take_along_axis(candidates, ranking, axis=1)
    available = jnp.sum(usable.astype(jnp.int32), axis=1)
    live_count = jax.random.randint(key_count, (boxes,), least, slot_count + 1)
    live_count = jnp.where(box_ids % 5 == 0, slot_count, live_count)
    live_count = jnp.minimum(live_count, available)
    slot_ids = jnp.arange(slot_count, dtype=jnp.int32)
    return jnp.where(slot_ids[None, :] < live_count[:, None], chosen, -1).astype(jnp.int32)


def level_lists(key, boxes, group_boxes):
    box_ids = jnp.arange(boxes, dtype=jnp.int32)
    first_candidate = (box_ids // group_boxes - 1) * group_boxes
    return pick_slots(key, first_candidate, 3 * group_boxes, CSLOTS, CSLOTS // 2, True)


def draw_near_list(key, part):
    key = jax.random.fold_in(key, 11)
    box_ids = jnp.arange(NLEAF, dtype=jnp.int32)
    others = pick_slots(key, box_ids - LEAF_DEV, 2 * LEAF_DEV + 1, NEAR - 1, NEAR // 2 - 1, False)
    return jnp.concatenate([box_ids[:, None], others], axis=1).astype(jnp.int32)


def draw_list_zero(key, part):
    key = jax.random.fold_in(key, 23)
    return level_lists(key, NLEAF, LEAF_DEV * N_LEAF)


def draw_list_one(key, part):
    key = jax.random.fold_in(key, 37)
    return level_lists(key, NLEAF // 2, LEAF_DEV // 2 * N_LEAF)


def draw_list_two(key, part):
    key = jax.random.fold_in(key, 41)
    return level_lists(key, NLEAF // 4, LEAF_DEV // 4 * N_LEAF)


def steps_of(key, shape, cuts, low, top_value):
    def one(position, blocks):
        draws = jax.random.uniform(jax.random.fold_in(jax.random.fold_in(key, 6), position), (blocks,), jnp.float32, low / len(cuts), top_value / len(cuts))
        return jnp.repeat(jnp.exp(draws), shape[position] // blocks).reshape((-1,) + (1,) * (len(shape) - position - 1))

    loudness = one(*cuts[0])
    for cut in cuts[1:]:
        loudness = loudness * one(*cut)
    return loudness


def gaussian(rng, extent, spread, most, cuts=(), kind=jnp.bfloat16):
    gain = steps_of(rng, extent, cuts, -0.22, 0.18) if cuts else 1.0
    array = jax.random.normal(rng, extent, jnp.float32) * spread * gain
    return jnp.minimum(jnp.maximum(array, -most), most).astype(kind)


def setup_inputs(seed: int = 0) -> dict:
    seeds = jax.random.split(jax.random.key(seed), 13)
    return {
        "sources": gaussian(seeds[0], (RHS, NPTS), 1.0, 6.0, ((1, 32),)),
        "points": gaussian(seeds[1], (3, NPTS), 1.0, 4.0, ((1, 32),)),
        "basis": gaussian(seeds[2], (NLEAF, RANK, LEAFPTS), LEAFPTS ** -0.5, 0.375, ((0, 32),)),
        "transfer_one": gaussian(seeds[3], (NLEAF, RANK * RANK), (2 * RANK) ** -0.5, 0.5, ((0, 32),)),
        "transfer_two": gaussian(seeds[4], (NBOX1, RANK * RANK), (2 * RANK) ** -0.5, 0.5, ((0, 32),)),
        "near_list": draw_near_list(jax.random.fold_in(seeds[12], 71), 0),
        "couple_zero": gaussian(seeds[6], (NLEAF, CSLOTS, RANK * RANK), (RANK * CSLOTS) ** -0.5, 0.125, ((0, 32),)),
        "couple_one": gaussian(seeds[7], (NBOX1, CSLOTS, RANK * RANK), (RANK * CSLOTS) ** -0.5, 0.125, ((0, 32),)),
        "couple_two": gaussian(seeds[8], (NBOX2, CSLOTS, RANK * RANK), (RANK * CSLOTS) ** -0.5, 0.125, ((0, 32),)),
        "list_zero": draw_list_zero(jax.random.fold_in(seeds[12], 71), 0),
        "list_one": draw_list_one(jax.random.fold_in(seeds[12], 71), 0),
        "list_two": draw_list_two(jax.random.fold_in(seeds[12], 71), 0),
    }


delta_sq = 0.01

def near_leaf(coords, values, near_list, leaf_index, scale_factor):
    entries = near_list[leaf_index]
    is_valid = entries >= 0
    safe_index = jnp.where(is_valid, entries, leaf_index).astype(jnp.int32)
    target = coords[:, leaf_index, :]
    source = coords[:, safe_index, :]
    distance = jnp.zeros((target.shape[1], safe_index.shape[0], source.shape[2]), jnp.float32)
    for component in range(3):
        difference = target[component][:, None, None] - source[component][None, :, :]
        distance = distance + difference * difference
    kernel = scale_factor * lax.rsqrt(distance + delta_sq) * is_valid.astype(jnp.float32)[None, :, None]
    kernel = kernel.astype(jnp.bfloat16).reshape(target.shape[1], -1)
    gathered = values[:, safe_index, :].reshape(values.shape[0], -1)
    return lax.dot_general(gathered, kernel, (((1,), (1,)), ((), ())), preferred_element_type=jnp.float32)

def couple_level(coeffs, matrices, lists):

    def one_box(box_index):
        entries = lists[box_index]
        is_valid = entries >= 0
        safe_index = jnp.where(is_valid, entries, 0).astype(jnp.int32)
        picked = coeffs[:, safe_index, :].astype(jnp.float32) * is_valid.astype(jnp.float32)[None, :, None]
        blocks = matrices[box_index].astype(jnp.float32).reshape(entries.shape[0], RANK, RANK)
        return jnp.einsum('rsj,skj->rk', picked, blocks)
    outcome = lax.map(one_box, jnp.arange(lists.shape[0], dtype=jnp.int32))
    return jnp.transpose(outcome, (1, 0, 2))

def upward(lower, transfer):
    right_count = lower.shape[0]
    boxes = lower.shape[1] // 2
    children = lower.astype(jnp.float32).reshape(right_count, boxes, 2, RANK)
    matrices = transfer.astype(jnp.float32).reshape(boxes, 2, RANK, RANK)
    return jnp.einsum('rbcj,bckj->rbk', children, matrices).astype(jnp.bfloat16)

def downward(far_terms, upper, transfer):
    right_count = upper.shape[0]
    boxes = upper.shape[1]
    matrices = transfer.astype(jnp.float32).reshape(boxes, 2, RANK, RANK)
    spread_down = jnp.einsum('rbk,bckj->rbcj', upper.astype(jnp.float32), matrices)
    return (far_terms + spread_down.reshape(right_count, 2 * boxes, RANK)).astype(jnp.bfloat16)

def reference(sources, points, basis, transfer_one, transfer_two, near_list, couple_zero, couple_one, couple_two, list_zero, list_one, list_two):
    right_count = sources.shape[0]
    values = sources.reshape(right_count, NLEAF, LEAFPTS)
    coords = points.astype(jnp.float32).reshape(3, NLEAF, LEAFPTS)
    scale_factor = 1.0 / math.sqrt(NEAR * LEAFPTS)
    near_terms = lax.map(lambda leaf_index: near_leaf(coords, values, near_list, leaf_index, scale_factor), jnp.arange(NLEAF, dtype=jnp.int32))
    level_zero = jnp.einsum('rbp,bkp->rbk', values.astype(jnp.float32), basis.astype(jnp.float32)).astype(jnp.bfloat16)
    level_one = upward(level_zero, transfer_one)
    level_two = upward(level_one, transfer_two)
    far_zero = couple_level(level_zero, couple_zero, list_zero)
    far_one = couple_level(level_one, couple_one, list_one)
    far_two = couple_level(level_two, couple_two, list_two)
    down_two = far_two.astype(jnp.bfloat16)
    down_one = downward(far_one, down_two, transfer_two)
    down_zero = downward(far_zero, down_one, transfer_one)
    far_part = jnp.einsum('rbk,bkp->rbp', down_zero.astype(jnp.float32), basis.astype(jnp.float32))
    total = jnp.transpose(near_terms, (1, 0, 2)) + far_part
    return total.reshape(right_count, NPTS).astype(jnp.bfloat16)
```

```python
import functools
import math

import jax
import jax.numpy as jnp
from jax import lax
from jax.experimental import pallas as pl
from jax.experimental.pallas import tpu as pltpu
from jax.sharding import PartitionSpec as P

delta_sq = 0.01
BF = jnp.bfloat16
F32 = jnp.float32
LANES = 128
COORD = 64.0
HALF = 8
UNROLL = 2 * HALF
SMEM = pltpu.SMEM
VMEM = pltpu.VMEM
LAST = (((1,), (1,)), ((), ()))


def dot(a, b):
    return jnp.dot(a, b, preferred_element_type=F32)


def dot_last(a, b):
    return lax.dot_general(a, b, LAST, preferred_element_type=F32)


def swap_halves(x):
    half = x.shape[1] // 2
    return jnp.concatenate([x[:, half:], x[:, :half]], axis=1)


def spread_pair(pair):
    lane = lax.broadcasted_iota(jnp.int32, pair.shape, 1)
    low = lane < pair.shape[1] // 2
    zero = jnp.zeros_like(pair)
    turned = swap_halves(pair)
    first = jnp.concatenate([jnp.where(low, pair, zero), jnp.where(low, zero, turned)], axis=0)
    second = jnp.concatenate([jnp.where(low, turned, zero), jnp.where(low, zero, pair)], axis=0)
    return first, second


def parity_matrix(half, parity, dtype=BF):
    row = lax.broadcasted_iota(jnp.int32, (half, 2 * half), 0)
    col = lax.broadcasted_iota(jnp.int32, (half, 2 * half), 1)
    return jnp.where(col == 2 * row + parity, 1.0, 0.0).astype(dtype)


def rows_by_box(flat):
    half = flat.shape[1] // LANES
    parts = jnp.stack([flat[:, q * LANES : (q + 1) * LANES] for q in range(half)], axis=0)
    return jnp.swapaxes(parts, 0, 1)


def peer(index, step, count):
    return index ^ step if count & (count - 1) == 0 else (step - index) % count


def up_kernel(
    members,
    near_smem,
    list0,
    list1,
    list2,
    src,
    basis,
    tr1,
    tr2,
    level_out,
    own_out,
    halo_out,
    count_out,
    tl0,
    tl1,
    tl2,
):
    leaves, slots = near_smem.shape
    rank = basis.shape[1]
    width = basis.shape[2]
    half = rank // 2
    boxes = leaves + leaves // 2 + leaves // 4
    dom = lax.axis_index("dom")
    leaf = lax.axis_index("leaf")

    zero_box = 3 * members * boxes
    offset = 0
    for lst, out, n in ((list0, tl0, leaves), (list1, tl1, leaves // 2), (list2, tl2, leaves // 4)):
        entry = lst[...]
        rel = entry - (dom - 1) * (members * n)
        unit = jnp.zeros_like(rel)
        for t in range(1, 3 * members):
            unit = unit + (rel >= t * n).astype(jnp.int32)
        local = rel - unit * n
        ring = (unit >= members).astype(jnp.int32) + (unit >= 2 * members).astype(jnp.int32)
        lf = unit - ring * members
        if members & (members - 1) == 0:
            place = lf ^ leaf
        else:
            place = lf + leaf
            place = place - jnp.where(place >= members, members, 0)
        spot = (ring * members + place) * boxes + offset + local
        out[...] = jnp.where(entry >= 0, spot, zero_box)
        offset += n

    first = (dom * members + leaf) * leaves

    def scan(b, carry):
        po, ph = carry
        for t in range(slots):
            e = near_smem[b, t]
            rel = e - first
            valid = e >= 0
            own = valid & (rel >= 0) & (rel < leaves)
            halo = valid & jnp.logical_not(own)
            own_out[po] = b * 128 + rel
            halo_out[ph] = b * 128 + jnp.where(rel < 0, rel + leaves, rel)
            po = po + own.astype(jnp.int32)
            ph = ph + halo.astype(jnp.int32)
        return po, ph

    for t in range(HALF):
        own_out[t] = leaves * 128
        halo_out[t] = leaves * 128
    po, ph = lax.fori_loop(0, leaves, scan, (jnp.int32(HALF), jnp.int32(HALF)))
    for t in range(UNROLL + HALF):
        own_out[po + t] = leaves * 128
        halo_out[ph + t] = leaves * 128
    count_out[0] = (po + UNROLL - 1) // UNROLL
    count_out[1] = (ph + UNROLL - 1) // UNROLL

    par = [parity_matrix(half, 0), parity_matrix(half, 1)]

    def raise_level(pairs, mats):
        found = []
        for p, pair in enumerate(pairs):
            e0, e1 = spread_pair(pair)
            wide = jnp.concatenate([e0, e1], axis=1)
            mat = jnp.concatenate([mats[2 * p], mats[2 * p + 1]], axis=1)
            found.append(dot_last(wide, mat).astype(BF))
        rhs = pairs[0].shape[0]
        up = [jnp.concatenate([f[c * rhs : (c + 1) * rhs] for f in found], axis=0) for c in range(2)]
        nat = dot(up[0], par[0]) + dot(up[1], par[1])
        nat = nat.astype(BF)
        return [
            jnp.concatenate(
                [nat[2 * p * rhs : (2 * p + 1) * rhs], nat[(2 * p + 1) * rhs : (2 * p + 2) * rhs]],
                axis=1,
            )
            for p in range(len(pairs) // 2)
        ]

    pairs0 = []
    for p in range(leaves // 2):
        parts = [
            dot_last(src[:, b * width : (b + 1) * width], basis[b]) for b in (2 * p, 2 * p + 1)
        ]
        pairs0.append(jnp.concatenate(parts, axis=1).astype(BF))
    pairs1 = raise_level(pairs0, rows_by_box(tr1[...]))
    pairs2 = raise_level(pairs1, rows_by_box(tr2[...]))
    for p, pair in enumerate(pairs0 + pairs1 + pairs2):
        level_out[p] = pair


def features(points, raw, target):
    x = points.astype(F32) * COORD
    square = x * x
    rest = square[0:1] + square[1:2] + square[2:3]
    lanes = x.shape[1]
    if target:
        rest = rest + delta_sq * COORD * COORD
        raw[0:3, :] = -2.0 * x
        at_parts, at_ones = 3, 6
    else:
        raw[0:3, :] = x
        at_parts, at_ones = 6, 3
    for k in range(3):
        part = rest.astype(BF).astype(F32)
        raw[at_parts + k : at_parts + k + 1, :] = part
        rest = rest - part
    raw[at_ones : at_ones + 3, :] = jnp.ones((3, lanes), F32)
    raw[9:16, :] = jnp.zeros((7, lanes), F32)


def target_features(points, raw, ft, width):
    features(points, raw, True)
    count = points.shape[1] // width
    for b in range(count):
        ft[b, 0:16, :] = raw[:, b * width : (b + 1) * width].astype(BF)
        ft[b, 16:, :] = jnp.zeros((LANES - 16, width), BF)
    ft[count] = jnp.zeros((LANES, width), BF)


def source_features(points, raw, fs, base, width):
    features(points, raw, False)
    for b in range(points.shape[1] // width):
        rows = raw[:, b * width : (b + 1) * width]
        rows = jnp.concatenate([rows, jnp.zeros((LANES - 16, width), F32)], axis=0)
        fs[base + b * width : base + (b + 1) * width, :] = jnp.transpose(rows).astype(BF)


def pair_loop(count, lst, ft, fs, values, acc, held, width):
    def block(code):
        b = code // 128
        g = code % 128
        near = dot(fs[pl.ds(pl.multiple_of(g * width, width), width), :], ft[b])
        return lax.rsqrt(near).astype(BF)

    def add(code, kernel):
        b = code // 128
        g = code % 128
        acc[b] += dot(values[:, pl.ds(pl.multiple_of(g * width, width), width)], kernel)

    held[...] = jnp.zeros_like(held)

    def body(n, carry):
        for h in range(2):
            for u in range(HALF):
                at = n * UNROLL + h * HALF + u
                add(lst[at], held[(1 - h) * HALF + u])
                held[h * HALF + u] = block(lst[at + HALF])
        return carry

    lax.fori_loop(0, count, body, 0)


def near_own_kernel(width, count, lst, points, values, acc, raw, ft, fs, held):
    acc[...] = jnp.zeros_like(acc)
    target_features(points[...], raw, ft, width)
    source_features(points[...], raw, fs, 0, width)
    pair_loop(count[0], lst, ft, fs, values, acc, held, width)


def near_halo_kernel(width, count, lst, points, left, right, acc_in, acc, raw, ft, fs, held, values):
    rhs = left.shape[0] - 3
    span = left.shape[1]
    acc[...] = acc_in[...]
    target_features(points[...], raw, ft, width)
    for k, side in enumerate((left, right)):
        source_features(side[rhs:, :], raw, fs, k * span, width)
        values[:, k * span : (k + 1) * span] = side[:rhs, :]
    pair_loop(count[1], lst, ft, fs, values, acc, held, width)


CHUNK = 3


def far_kernel(
    factor,
    tl0,
    tl1,
    tl2,
    lv_left,
    lv_own,
    lv_right,
    tr1,
    tr2,
    basis,
    acc,
    cp0,
    cp1,
    cp2,
    out,
    wide,
    mats,
    found,
    sems,
):
    members, pairs = lv_own.shape[0], lv_own.shape[1]
    boxes = 2 * pairs
    leaves, rank, width = basis.shape
    half = rank // 2
    rhs = lv_own.shape[2]
    slots = tl0.shape[1]
    levels = ((cp2, tl2, leaves + leaves // 2), (cp1, tl1, leaves), (cp0, tl0, 0))

    copies = []
    for cp, tl, base in levels:
        for k in range(cp.shape[0] // CHUNK):
            at = base + k * CHUNK
            copies.append(
                pltpu.make_async_copy(
                    cp.at[pl.ds(k * CHUNK, CHUNK)], mats.at[pl.ds(at, CHUNK)], sems.at[at // CHUNK]
                )
            )
    for copy in copies:
        copy.start()

    wide[3 * members * boxes] = jnp.zeros((2 * rhs, LANES), BF)
    for s, lv in enumerate((lv_left, lv_own, lv_right)):

        def widen(m, carry):
            for p in range(pairs):
                e0, e1 = spread_pair(lv[m, p])
                at = (s * members + m) * boxes + 2 * p
                wide[at] = e0
                wide[at + 1] = e1
            return carry

        lax.fori_loop(0, members, widen, 0)

    for cp, tl, base in levels:

        def chunk(n, carry):
            at = base + n * CHUNK
            pltpu.make_async_copy(
                cp.at[pl.ds(n * CHUNK, CHUNK)], mats.at[pl.ds(at, CHUNK)], sems.at[at // CHUNK]
            ).wait()
            rows = [rows_by_box(mats[at + u]) for u in range(CHUNK)]
            sums = []
            for u in range(CHUNK):
                total = None
                for s in range(0, slots, 2):
                    co = jnp.concatenate(
                        [wide[tl[n * CHUNK + u, s]], wide[tl[n * CHUNK + u, s + 1]]], axis=1
                    )
                    mat = jnp.concatenate([rows[u][s], rows[u][s + 1]], axis=1)
                    term = dot_last(co, mat)
                    total = term if total is None else total + term
                sums.append(total)
            for u in range(CHUNK):
                found[at + u] = sums[u]
            return carry

        lax.fori_loop(0, cp.shape[0] // CHUNK, chunk, 0)

    par = [parity_matrix(half, 0), parity_matrix(half, 1)]

    def natural(base, n):
        total = None
        for c in range(2):
            part = found[base : base + n, c * rhs : (c + 1) * rhs, :].reshape(n * rhs, half)
            high = part.astype(BF)
            low = (part - high.astype(F32)).astype(BF)
            term = dot(high, par[c]) + dot(low, par[c])
            total = term if total is None else total + term
        return total

    def lower(far, upper, mat, n):
        result = []
        for b in range(n):
            for c in range(2):
                x = dot(upper[b], mat[2 * b + c])
                spread = x[:rhs, :rank] + x[rhs:, rank:]
                at = (2 * b + c) * rhs
                result.append((far[at : at + rhs] + spread).astype(BF))
        return result

    top = leaves // 4
    base2 = leaves + leaves // 2
    down_two = [found[base2 + b].astype(BF) for b in range(top)]
    far_one = natural(leaves, leaves // 2)
    far_zero = natural(0, leaves)
    down_one = lower(far_one, down_two, rows_by_box(tr2[...]), top)
    stacked = jnp.concatenate(down_one, axis=0)
    split = [dot_last(stacked, par[c]).astype(BF) for c in range(2)]
    down_one_split = [
        jnp.concatenate([split[c][b * rhs : (b + 1) * rhs] for c in range(2)], axis=0)
        for b in range(leaves // 2)
    ]
    down_zero = lower(far_zero, down_one_split, rows_by_box(tr1[...]), leaves // 2)
    for b in range(leaves):
        total = acc[b] * factor + dot(down_zero[b], basis[b])
        out[:, b * width : (b + 1) * width] = total.astype(BF)


def params(megabytes):
    return pltpu.CompilerParams(vmem_limit_bytes=megabytes << 20)


def cost(flops, nbytes):
    return pl.CostEstimate(flops=flops, bytes_accessed=nbytes, transcendentals=0)


def shards(
    sources,
    points,
    basis,
    transfer_one,
    transfer_two,
    near_list,
    couple_zero,
    couple_one,
    couple_two,
    list_zero,
    list_one,
    list_two,
):
    rhs, span = sources.shape
    leaves, rank, width = basis.shape
    slots = near_list.shape[1]
    members = lax.axis_size("leaf")
    groups = lax.axis_size("dom")
    devices = members * groups
    pairs = (leaves + leaves // 2 + leaves // 4) // 2
    boxes = 2 * pairs
    half = rank // 2
    smem = pl.BlockSpec(memory_space=SMEM)
    vmem = pl.BlockSpec(memory_space=VMEM)
    hbm = pl.BlockSpec(memory_space=pl.ANY)
    sds = jax.ShapeDtypeStruct
    both = ("dom", "leaf")

    stacked = jnp.concatenate([sources, points], axis=0)
    left = lax.ppermute(stacked, both, [(i, i + 1) for i in range(devices - 1)])
    right = lax.ppermute(stacked, both, [(i + 1, i) for i in range(devices - 1)])

    list_size = leaves * slots + UNROLL + 2 * HALF
    level, own_pairs, halo_pairs, counts, tl0, tl1, tl2 = pl.pallas_call(
        functools.partial(up_kernel, members),
        name="upward",
        in_specs=[smem] + [vmem] * 7,
        out_specs=[vmem, smem, smem, smem, vmem, vmem, vmem],
        out_shape=[
            sds((pairs, rhs, 2 * rank), BF),
            sds((list_size,), jnp.int32),
            sds((list_size,), jnp.int32),
            sds((2,), jnp.int32),
            sds(list_zero.shape, jnp.int32),
            sds(list_one.shape, jnp.int32),
            sds(list_two.shape, jnp.int32),
        ],
        compiler_params=params(24),
        cost_estimate=cost(100_000_000, 10_000_000),
    )(near_list, list_zero, list_one, list_two, sources, basis, transfer_one, transfer_two)

    pieces = [level]
    for step in range(1, members):
        pieces.append(
            lax.ppermute(level, "leaf", [(i, peer(i, step, members)) for i in range(members)])
        )

    acc_shape = sds((leaves + 1, rhs, width), F32)
    near_scratch = [
        pltpu.VMEM((16, span), F32),
        pltpu.VMEM((leaves + 1, LANES, width), BF),
    ]
    acc = pl.pallas_call(
        functools.partial(near_own_kernel, width),
        name="near_own",
        in_specs=[smem, smem, vmem, vmem],
        out_specs=vmem,
        out_shape=acc_shape,
        scratch_shapes=near_scratch
        + [pltpu.VMEM((span, LANES), BF), pltpu.VMEM((UNROLL, width, width), BF)],
        compiler_params=params(32),
        cost_estimate=cost(5_000_000_000, 30_000_000),
    )(counts, own_pairs, points, sources)

    joined = jnp.stack(pieces, axis=0)
    acc, halo_pairs, joined = lax.optimization_barrier((acc, halo_pairs, joined))
    lv_left = lax.ppermute(joined, "dom", [(i, i + 1) for i in range(groups - 1)])
    lv_right = lax.ppermute(joined, "dom", [(i + 1, i) for i in range(groups - 1)])

    acc = pl.pallas_call(
        functools.partial(near_halo_kernel, width),
        name="near_halo",
        in_specs=[smem, smem, vmem, vmem, vmem, vmem],
        out_specs=vmem,
        out_shape=acc_shape,
        scratch_shapes=near_scratch
        + [
            pltpu.VMEM((2 * span, LANES), BF),
            pltpu.VMEM((UNROLL, width, width), BF),
            pltpu.VMEM((rhs, 2 * span), BF),
        ],
        compiler_params=params(32),
        cost_estimate=cost(5_000_000_000, 30_000_000),
    )(counts, halo_pairs, points, left, right, acc)

    factor = COORD / math.sqrt(slots * width)
    return pl.pallas_call(
        functools.partial(far_kernel, factor),
        name="far",
        in_specs=[smem] * 3 + [vmem] * 7 + [hbm] * 3,
        out_specs=vmem,
        out_shape=sds((rhs, span), BF),
        scratch_shapes=[
            pltpu.VMEM((3 * members * boxes + 1, 2 * rhs, LANES), BF),
            pltpu.VMEM((boxes,) + couple_zero.shape[1:], BF),
            pltpu.VMEM((boxes, 2 * rhs, half), F32),
            pltpu.SemaphoreType.DMA((boxes // CHUNK,)),
        ],
        compiler_params=params(60),
        cost_estimate=cost(5_000_000_000, 30_000_000),
    )(
        tl0,
        tl1,
        tl2,
        lv_left,
        joined,
        lv_right,
        transfer_one,
        transfer_two,
        basis,
        acc,
        couple_zero,
        couple_one,
        couple_two,
    )


def solution(mesh):
    row = P(None, ("dom", "leaf"))
    two = P(("dom", "leaf"), None)
    three = P(("dom", "leaf"), None, None)
    placed = (row, row, three, two, two, two, three, three, three, two, two, two)
    return jax.shard_map(shards, mesh=mesh, in_specs=placed, out_specs=row, check_vma=False)
```
